512 devices in a mesh: chan: 64 (over y, z_hi, core), day: 8 (over x, z_lo).
Axes of the slice: x: 4, y: 8, z: 8 (z_hi: 4, z_lo: 2; z = z_hi * 2 + z_lo), core: 2. Of those that a mesh axis runs over, the one named last changes fastest.
Arguments:
- recordings: bfloat16 [8, 4096, 8, 1024], P('day', 'chan'), may hold values from -6 to 6
- good_windows: int32 [8, 4096, 8], P('day', 'chan'), may hold values 0 or 1
- response: float32 [256], replicated, may hold values from 0.3 to 3
Outputs:
- correlations: float32 [4096, 2, 64, 128], P(('chan', 'day'))
The draws below stay inside these ranges and needn't reach their ends.
All inputs are finite; a program needn't handle non-finite values. No bound on the sum of `good_windows` on one device may be relied on, other than what follows from the above.
Results may differ from the reference program's by a relative error of at most 0.0076.
Values may be sent and summed in bfloat16 or wider, within the bound.
No kernel may reach another device: no remote copies, remote signals or barrier semaphores. Data moves between devices by JAX's collectives and lax.ppermute only.
A program may use at most 64 MiB of HBM per device.

```python
import math
import jax
import jax.numpy as jnp
from jax import lax

CB = 64
DAY_DEV = 1
W = 8
S = 1024
F = 256
FIRST_BIN = 4
L = 128
ROUNDS = 2
CHANNELS = 4096
DAYS = 8
N_CHAN = 64
N_DAY = 8


def plant(entries, own_key, least, high):
    longest = entries.shape.index(max(entries.shape))
    spots = []
    for shift in (0, 1):
        where = [jax.random.randint(jax.random.fold_in(own_key, axis), (), 0, length) for axis, length in enumerate(entries.shape)]
        where[longest] = (where[longest] + shift) % entries.shape[longest]
        spots.append(tuple(where))
    return entries.at[spots[0]].set(least).at[spots[1]].set(high)


def block_levels(rng, shape, split, smallest, largest):
    factor_of = 1.0
    for axis_at, parts in split:
        draws = jax.random.uniform(jax.random.fold_in(jax.random.fold_in(rng, 6), axis_at), (parts,), jnp.float32, smallest / len(split), largest / len(split))
        factor_of = factor_of * jnp.repeat(jnp.exp(draws), shape[axis_at] // parts).reshape((-1,) + (1,) * (len(shape) - 1 - axis_at))
    return factor_of


def scatter_about(key, dims, scale, bound, split=(), kind=jnp.bfloat16):
    values = jax.random.normal(key, dims, jnp.float32) * scale
    if len(split) > 0:
        values = block_levels(key, dims, split, -0.22, 0.18) * values
    return jnp.clip(values, min=-bound, max=bound).astype(kind)


def setup_inputs(seed: int = 0) -> dict:
    seeds = jax.random.split(jax.random.key(seed), 4)
    recordings = scatter_about(seeds[0], (DAYS, CHANNELS, W, S), 1.0, 6.0, ((0, 8), (1, 64)))
    good_windows = plant((jax.random.randint(seeds[1], (DAYS, CHANNELS, W), 0, 8) < 7).astype(jnp.int32), jax.random.fold_in(seeds[1], 1), 0, 1)
    response = jnp.clip(jnp.exp(jax.random.uniform(seeds[2], (F,), jnp.float32, math.log(0.3), math.log(3.0))), 0.3, 3.0)
    return {"recordings": recordings, "good_windows": good_windows, "response": response}


def dft_table(samples, bin_count, first_bin):
    sample_index = jnp.arange(samples, dtype=jnp.int32)
    bin_index = jnp.arange(bin_count, dtype=jnp.int32) + first_bin
    phase_int = jnp.mod(sample_index[:, None] * bin_index[None, :], samples)
    phase = phase_int.astype(jnp.float32) * (2.0 * math.pi / samples)
    return jnp.concatenate([jnp.cos(phase), -jnp.sin(phase)], axis=1).astype(jnp.bfloat16)

def lag_table(samples, bin_count, first_bin, lag_count):
    bin_index = jnp.arange(bin_count, dtype=jnp.int32) + first_bin
    shift_index = jnp.arange(lag_count, dtype=jnp.int32) - lag_count // 2
    phase_int = jnp.mod(bin_index[:, None] * shift_index[None, :], samples)
    phase = phase_int.astype(jnp.float32) * (2.0 * math.pi / samples)
    return jnp.concatenate([jnp.cos(phase), -jnp.sin(phase)], axis=0).astype(jnp.bfloat16)

def band_spectra(recordings, good_windows, response):
    samples = recordings.shape[-1]
    bin_count = response.shape[0]
    values = recordings.astype(jnp.float32)
    power = lax.optimization_barrier(jnp.mean(values * values, axis=-1, keepdims=True))
    normed = (values * lax.rsqrt(power + 1e-06)).astype(jnp.bfloat16)
    flat = normed.reshape(-1, samples)
    spectra = jnp.dot(flat, dft_table(samples, bin_count, FIRST_BIN), preferred_element_type=jnp.float32)
    spectra = spectra.reshape(recordings.shape[:-1] + (2 * bin_count,))
    weight = good_windows.astype(jnp.float32)[..., None] * jnp.concatenate([response, response])
    return (spectra * weight).astype(jnp.bfloat16)

def cross_lags(mine, partner, table):
    bin_count = mine.shape[-1] // 2
    mine_re = mine[..., :bin_count].astype(jnp.float32)
    mine_im = mine[..., bin_count:].astype(jnp.float32)
    part_re = partner[..., :bin_count].astype(jnp.float32)
    part_im = partner[..., bin_count:].astype(jnp.float32)
    high = lax.Precision.HIGHEST
    real_part = jnp.einsum('dixf,djxf->ijf', mine_re, part_re, precision=high) + jnp.einsum('dixf,djxf->ijf', mine_im, part_im, precision=high)
    imag_part = jnp.einsum('dixf,djxf->ijf', mine_im, part_re, precision=high) - jnp.einsum('dixf,djxf->ijf', mine_re, part_im, precision=high)
    stacked = jnp.concatenate([real_part, imag_part], axis=-1).astype(jnp.bfloat16)
    chans = stacked.shape[0]
    lag_sums = jnp.dot(stacked.reshape(-1, 2 * bin_count), table, preferred_element_type=jnp.float32)
    return lag_sums.reshape(chans, chans, -1)

def reference(recordings, good_windows, response):
    blocks = N_CHAN
    shaped = jnp.moveaxis(recordings.reshape(DAYS, blocks, CB, W, S), 1, 0)
    mask_shaped = jnp.moveaxis(good_windows.reshape(DAYS, blocks, CB, W), 1, 0)
    spectra = lax.map(lambda pair: band_spectra(pair[0], pair[1], response), (shaped, mask_shaped))
    table = lag_table(S, F, FIRST_BIN, L)

    def one_block(block):
        mine = spectra[block].reshape(N_DAY, DAY_DEV, CB, W, 2 * F)
        rounds_out = []
        for round_index in range(ROUNDS):
            partner_index = jnp.mod(block + (round_index + 1), blocks).astype(jnp.int32)
            partner = spectra[partner_index].reshape(N_DAY, DAY_DEV, CB, W, 2 * F)
            per_group = jax.vmap(lambda first, second: cross_lags(first, second, table))(mine, partner)
            rounds_out.append(lax.optimization_barrier(jnp.sum(per_group, axis=0)))
        return jnp.stack(rounds_out, axis=1)
    result = lax.map(one_block, jnp.arange(blocks, dtype=jnp.int32))
    return result.reshape(CHANNELS, ROUNDS, CB, L)
```

```python
import functools
import math

import jax
import jax.numpy as jnp
import ml_dtypes
import numpy as np
from jax import lax
from jax.experimental import pallas as pl
from jax.experimental.pallas import tpu as pltpu
from jax.sharding import PartitionSpec as P

FIRST_BIN = 4
S = 1024
F = 256
L = 128
CB = 64
W = 8
DAYS = 8
FS = F // DAYS
VMEM = 40 * 1024 * 1024


def phase_table(product):
    phase = np.mod(product, S).astype(np.float32) * np.float32(2.0 * math.pi / S)
    return np.cos(phase), -np.sin(phase)


def dft_table():
    bins = np.arange(F) + FIRST_BIN
    re, im = phase_table(bins[:, None] * np.arange(S)[None, :])
    return np.concatenate([re, im], axis=0).astype(ml_dtypes.bfloat16)


def lag_table():
    bins = np.arange(F) + FIRST_BIN
    re, im = phase_table(bins[:, None] * (np.arange(L) - L // 2)[None, :])
    return np.concatenate([re, im], axis=0).astype(ml_dtypes.bfloat16)


def lower_half(shape):
    return lax.broadcasted_iota(jnp.int32, shape, 1) < CB


def spectra_kernel(x_ref, good_ref, resp_ref, table_ref, out_ref, xs, normed):
    for lane in range(S // 128):
        xs[lane] = x_ref[:, 128 * lane : 128 * (lane + 1)].astype(jnp.float32)
    for w in range(W):
        rows = pl.ds(w, CB, stride=W)
        v = jnp.concatenate([xs[lane, rows, :] for lane in range(S // 128)], axis=1)
        power = jnp.mean(v * v, axis=-1, keepdims=True)
        normed[pl.ds(w * CB, CB), :] = (v * lax.rsqrt(power + 1e-06)).astype(jnp.bfloat16)
    gain = jnp.transpose(jnp.broadcast_to(resp_ref[...], (2 * CB, F)))
    low = lower_half((F, 2 * CB))
    good = good_ref[...].astype(jnp.float32)
    for half in range(2):
        rows = normed[pl.ds(half * 4 * CB, 4 * CB), :]
        spectra = lax.dot_general(
            table_ref[...], rows, (((1,), (1,)), ((), ())), preferred_element_type=jnp.float32
        )
        for pair in range(2):
            w = 4 * half + 2 * pair
            mask = jnp.concatenate([good[w : w + 1, :], good[w + 1 : w + 2, :]], axis=1)
            weight = gain * mask
            cols = slice(2 * CB * pair, 2 * CB * (pair + 1))
            re = spectra[:F, cols] * weight
            im = spectra[F:, cols] * weight
            first = jnp.where(low, re, pltpu.roll(im, CB, 1))
            second = jnp.where(low, pltpu.roll(re, CB, 1), im)
            out_ref[:, w] = first.astype(jnp.bfloat16).reshape(DAYS, FS, 2 * CB)
            out_ref[:, w + 1] = second.astype(jnp.bfloat16).reshape(DAYS, FS, 2 * CB)


def cross_kernel(mine_ref, one_ref, two_ref, out_ref, wide):
    for at, ref in enumerate((mine_ref, one_ref, two_ref)):
        wide[at] = ref[...].astype(jnp.float32)
    low = lower_half((DAYS * W, 2 * CB))
    for f in range(FS):
        rows = pl.ds(f, DAYS * W, stride=FS)
        mine, one, two = wide[0, rows, :], wide[1, rows, :], wide[2, rows, :]
        turned = pltpu.roll(mine, CB, 1)
        left = jnp.concatenate([mine, jnp.where(low, turned, -turned)], axis=0)
        right = jnp.concatenate(
            [
                jnp.where(low, one, pltpu.roll(two, CB, 1)),
                jnp.where(low, pltpu.roll(one, CB, 1), two),
            ],
            axis=0,
        )
        cross = lax.dot_general(
            left.astype(jnp.bfloat16),
            right.astype(jnp.bfloat16),
            (((0,), (0,)), ((), ())),
            preferred_element_type=jnp.float32,
        )
        for k in range(DAYS):
            piece = jnp.concatenate([cross[8 * k : 8 * k + 8], cross[CB + 8 * k : CB + 8 * k + 8]], axis=0)
            out_ref[k, f] = piece.astype(jnp.bfloat16)


def lag_kernel(cross_ref, table_ref, out_ref, wide):
    wide[...] = cross_ref[...].astype(jnp.float32)
    for i in range(8):
        parts = [wide[pl.ds(c * 8 + i, F, stride=16), :] for c in range(2)]
        left = jnp.concatenate(parts, axis=0).astype(jnp.bfloat16)
        out_ref[i] = lax.dot_general(
            left, table_ref[...], (((0,), (0,)), ((), ())), preferred_element_type=jnp.float32
        )


def call(kernel, out_shape, dtype, scratch, flops, *args):
    return pl.pallas_call(
        kernel,
        out_shape=jax.ShapeDtypeStruct(out_shape, dtype),
        in_specs=[pl.BlockSpec(memory_space=pltpu.VMEM)] * len(args),
        out_specs=pl.BlockSpec(memory_space=pltpu.VMEM),
        scratch_shapes=scratch,
        compiler_params=pltpu.CompilerParams(vmem_limit_bytes=VMEM),
        cost_estimate=pl.CostEstimate(flops=flops, bytes_accessed=2 << 20, transcendentals=0),
    )(*args)


def shards(recordings, good_windows, response):
    blocks = lax.axis_size("chan")
    core = lax.rem(lax.axis_index("chan"), 2)
    x = recordings.reshape(CB * W, S)
    good = jnp.transpose(good_windows, (0, 2, 1)).reshape(W, CB)
    spectra = call(
        spectra_kernel, (DAYS, W, FS, 2 * CB), jnp.bfloat16,
        [pltpu.VMEM((S // 128, CB * W, 128), jnp.float32), pltpu.VMEM((CB * W, S), jnp.bfloat16)],
        2 * CB * W * S * 2 * F, x, good, response.reshape(1, F), jnp.asarray(dft_table()),
    )
    mine = lax.all_to_all(spectra, "day", 0, 0, tiled=True)
    two = lax.ppermute(mine, "chan", [(b, (b - 2) % blocks) for b in range(blocks)])
    give = jnp.where(core == 0, two, mine)
    one = lax.ppermute(give, "chan", [(b, b ^ 1) for b in range(blocks)])
    cross = call(
        cross_kernel, (DAYS, FS, 16, 2 * CB), jnp.bfloat16,
        [pltpu.VMEM((3, DAYS * W * FS, 2 * CB), jnp.float32)],
        2 * FS * 128 * 128 * 128,
        *(v.reshape(DAYS * W * FS, 2 * CB) for v in (mine, one, two)),
    )
    cross = lax.all_to_all(cross, "day", 0, 0, tiled=True)
    lags = call(
        lag_kernel, (8, 2 * CB, L), jnp.float32,
        [pltpu.VMEM((F * 16, 2 * CB), jnp.float32)],
        2 * 8 * 128 * 512 * 128,
        cross.reshape(F * 16, 2 * CB), jnp.asarray(lag_table()),
    )
    return lags.reshape(8, 2, CB, L)


def solution(mesh):
    in_specs = (P("day", "chan", None, None), P("day", "chan", None), P())
    out_specs = P(("chan", "day"), None, None, None)
    return jax.shard_map(shards, mesh=mesh, in_specs=in_specs, out_specs=out_specs, check_vma=False)
```

```python
import math

import jax
import jax.numpy as jnp
import ml_dtypes
import numpy as np
from jax import lax
from jax.experimental import pallas as pl
from jax.experimental.pallas import tpu as pltpu
from jax.sharding import PartitionSpec as P

FIRST_BIN = 4
S = 1024
F = 256
L = 128
CB = 64
W = 8
DAYS = 8
FS = F // DAYS
ROWS = DAYS * W * FS
VMEM = 40 * 1024 * 1024


def phase_table(product):
    phase = np.mod(product, S).astype(np.float32) * np.float32(2.0 * math.pi / S)
    return np.concatenate([np.cos(phase), -np.sin(phase)], axis=0).astype(ml_dtypes.bfloat16)


def dft_table():
    return phase_table((np.arange(F) + FIRST_BIN)[:, None] * np.arange(S)[None, :])


def lag_table():
    return phase_table((np.arange(F) + FIRST_BIN)[:, None] * (np.arange(L) - L // 2)[None, :])


def low_lanes(rows):
    return lax.broadcasted_iota(jnp.int32, (rows, 2 * CB), 1) < CB


def turn(v):
    return pltpu.roll(v, CB, 1)


def spectra_kernel(x_ref, good_ref, resp_ref, table_ref, out_ref, xs, normed):
    lanes = S // 128
    for lane in range(lanes):
        xs[lane] = x_ref[:, 128 * lane : 128 * (lane + 1)].astype(jnp.float32)
    for w in range(W):
        rows = pl.ds(w, CB, stride=W)
        v = jnp.concatenate([xs[lane, rows, :] for lane in range(lanes)], axis=1)
        power = jnp.mean(v * v, axis=-1, keepdims=True)
        normed[pl.ds(w * CB, CB), :] = (v * lax.rsqrt(power + 1e-06)).astype(jnp.bfloat16)
    gain = jnp.transpose(jnp.broadcast_to(resp_ref[...], (2 * CB, F)))
    low = low_lanes(F)
    good = good_ref[...].astype(jnp.float32)
    for half in range(2):
        rows = normed[pl.ds(half * 4 * CB, 4 * CB), :]
        spectra = lax.dot_general(
            table_ref[...], rows, (((1,), (1,)), ((), ())), preferred_element_type=jnp.float32
        )
        for pair in range(2):
            w = 4 * half + 2 * pair
            mask = jnp.concatenate([good[w : w + 1, :], good[w + 1 : w + 2, :]], axis=1)
            weight = gain * mask
            cols = slice(2 * CB * pair, 2 * CB * (pair + 1))
            re = spectra[:F, cols] * weight
            im = spectra[F:, cols] * weight
            first = jnp.where(low, re, turn(im)).astype(jnp.bfloat16).reshape(DAYS, FS, 2 * CB)
            second = jnp.where(low, turn(re), im).astype(jnp.bfloat16).reshape(DAYS, FS, 2 * CB)
            for to in range(2):
                out_ref[to, :, w] = first
                out_ref[to, :, w + 1] = second


def cross_into(out_ref, left, right):
    low = low_lanes(DAYS * W)
    for pair in range(FS // 2):
        both = []
        for f in (2 * pair, 2 * pair + 1):
            rows = pl.ds(f, DAYS * W, stride=FS)
            one, two = left[rows, :], right[rows, :]
            lhs = jnp.concatenate([one, turn(one)], axis=0)[:, :CB].astype(jnp.bfloat16)
            rhs = jnp.concatenate([jnp.where(low, two, -two), turn(two)], axis=0).astype(jnp.bfloat16)
            both.append(
                lax.dot_general(lhs, rhs, (((0,), (0,)), ((), ())), preferred_element_type=jnp.float32)
            )
        for k in range(DAYS):
            piece = jnp.concatenate([v[8 * k : 8 * k + 8] for v in both], axis=0)
            out_ref[k, pl.ds(16 * pair, 16), :] = piece.astype(jnp.bfloat16)


def second_kernel(odd_ref, near_ref, swap_ref, out_ref, left, right):
    odd = odd_ref[0] == 1

    @pl.when(odd)
    def _():
        left[...] = swap_ref[...].astype(jnp.float32)
        right[...] = near_ref[1].astype(jnp.float32)

    @pl.when(jnp.logical_not(odd))
    def _():
        left[...] = near_ref[0].astype(jnp.float32)
        right[...] = swap_ref[...].astype(jnp.float32)

    cross_into(out_ref, left, right)


def first_kernel(odd_ref, near_ref, swap_ref, out_ref, left, right):
    odd = odd_ref[0] == 1

    @pl.when(odd)
    def _():
        left[...] = near_ref[0].astype(jnp.float32)
        right[...] = near_ref[1].astype(jnp.float32)

    @pl.when(jnp.logical_not(odd))
    def _():
        left[...] = near_ref[1].astype(jnp.float32)
        right[...] = swap_ref[...].astype(jnp.float32)

    cross_into(out_ref, left, right)


def lags_of(cross_ref, table_ref, wide):
    wide[...] = cross_ref[...].astype(jnp.float32)
    low = low_lanes(F)
    for pair in range(4):
        one, two = (wide[pl.ds(2 * pair + i, F, stride=8), :] for i in range(2))
        re = jnp.where(low, one, turn(two))
        im = jnp.where(low, turn(one), two)
        yield pair, lax.dot_general(
            jnp.concatenate([re, im], axis=0).astype(jnp.bfloat16), table_ref[...],
            (((0,), (0,)), ((), ())), preferred_element_type=jnp.float32,
        ).reshape(2, CB, L)


def second_lag_kernel(cross_ref, table_ref, out_ref, wide):
    for pair, lags in lags_of(cross_ref, table_ref, wide):
        out_ref[pl.ds(2 * pair, 2)] = lags.astype(jnp.bfloat16)


def first_lag_kernel(cross_ref, table_ref, second_ref, out_ref, wide):
    for pair, lags in lags_of(cross_ref, table_ref, wide):
        out_ref[pl.ds(2 * pair, 2), 0] = lags
    out_ref[:, 1] = second_ref[...].astype(jnp.float32)


def call(kernel, out_shape, dtype, scratch, flops, *args, scalars=0):
    smem = [pl.BlockSpec(memory_space=pltpu.SMEM)] * scalars
    return pl.pallas_call(
        kernel,
        out_shape=jax.ShapeDtypeStruct(out_shape, dtype),
        in_specs=smem + [pl.BlockSpec(memory_space=pltpu.VMEM)] * (len(args) - scalars),
        out_specs=pl.BlockSpec(memory_space=pltpu.VMEM),
        scratch_shapes=scratch,
        compiler_params=pltpu.CompilerParams(vmem_limit_bytes=VMEM),
        cost_estimate=pl.CostEstimate(flops=flops, bytes_accessed=2 << 20, transcendentals=0),
    )(*args)


WIDE = pltpu.VMEM((ROWS, 2 * CB), jnp.float32)
CROSS_FLOPS = 2 * FS * 64 * 128 * 128
LAG_FLOPS = 2 * 8 * 64 * 512 * 128
CROSS_SHAPE = (DAYS, FS * 8, 2 * CB)


def spectra_call(x, good, response):
    return call(
        spectra_kernel, (2, DAYS, W, FS, 2 * CB), jnp.bfloat16,
        [pltpu.VMEM((S // 128, CB * W, 128), jnp.float32), pltpu.VMEM((CB * W, S), jnp.bfloat16)],
        2 * CB * W * S * 2 * F, x, good, response, jnp.asarray(dft_table()),
    )


def second_call(flag, near, swap):
    return call(second_kernel, CROSS_SHAPE, jnp.bfloat16, [WIDE, WIDE], CROSS_FLOPS, flag, near, swap, scalars=1)


def first_call(flag, near, swap):
    return call(first_kernel, CROSS_SHAPE, jnp.bfloat16, [WIDE, WIDE], CROSS_FLOPS, flag, near, swap, scalars=1)


def second_lag_call(cross):
    return call(second_lag_kernel, (8, CB, L), jnp.bfloat16, [WIDE], LAG_FLOPS, cross, jnp.asarray(lag_table()))


def first_lag_call(cross, second):
    return call(
        first_lag_kernel, (8, 2, CB, L), jnp.float32, [WIDE], LAG_FLOPS, cross, jnp.asarray(lag_table()), second
    )


def shards(recordings, good_windows, response):
    blocks = lax.axis_size("chan")
    odd = lax.rem(lax.axis_index("chan"), 2)
    flag = odd.astype(jnp.int32).reshape(1)
    x = recordings.reshape(CB * W, S)
    good = jnp.transpose(good_windows, (0, 2, 1)).reshape(W, CB)
    spectra = spectra_call(x, good, response.reshape(1, F))
    groups = [
        [b % blocks * DAYS + d for b in (block, block + 1) for d in range(DAYS)]
        for block in range(1, blocks, 2)
    ]
    near = lax.all_to_all(
        spectra.reshape(2 * DAYS, W, FS, 2 * CB), ("chan", "day"), 0, 0, axis_index_groups=groups, tiled=True
    ).reshape(2, ROWS, 2 * CB)
    mine = jnp.where(odd == 1, near[0], near[1])
    swap = lax.ppermute(mine, "chan", [(b, b ^ 1) for b in range(blocks)])
    second = lax.all_to_all(second_call(flag, near, swap), "day", 0, 0, tiled=True)
    first = lax.all_to_all(first_call(flag, near, swap), "day", 0, 0, tiled=True)
    second = second_lag_call(second.reshape(F * 8, 2 * CB))
    second = lax.ppermute(second, "chan", [(b, (b - 1) % blocks) for b in range(blocks)])
    return first_lag_call(first.reshape(F * 8, 2 * CB), second)


def solution(mesh):
    in_specs = (P("day", "chan", None, None), P("day", "chan", None), P())
    out_specs = P(("chan", "day"), None, None, None)
    return jax.shard_map(shards, mesh=mesh, in_specs=in_specs, out_specs=out_specs, check_vma=False)
```

```python
import math

import jax
import jax.numpy as jnp
import ml_dtypes
import numpy as np
from jax import lax
from jax.experimental import pallas as pl
from jax.experimental.pallas import tpu as pltpu
from jax.sharding import PartitionSpec as P

FIRST_BIN = 4
S = 1024
F = 256
L = 128
CB = 64
W = 8
DAYS = 8
FS = F // DAYS
ROWS = DAYS * W * FS
VMEM = 24 * 1024 * 1024
PARTS = 4


def phase_table(product):
    phase = np.mod(product, S).astype(np.float32) * np.float32(2.0 * math.pi / S)
    return np.concatenate([np.cos(phase), -np.sin(phase)], axis=0).astype(ml_dtypes.bfloat16)


def dft_table():
    return phase_table((np.arange(F) + FIRST_BIN)[:, None] * np.arange(S)[None, :])


def lag_table():
    return phase_table((np.arange(F) + FIRST_BIN)[:, None] * (np.arange(L) - L // 2)[None, :])


def low_lanes(rows):
    return lax.broadcasted_iota(jnp.int32, (rows, 2 * CB), 1) < CB


def turn(v):
    return pltpu.roll(v, CB, 1)


def spectra_kernel(x_hbm, good_hbm, resp_hbm, table_hbm, out_ref, x_ref, good_ref, resp_ref, table_ref, xs, normed, sems):
    part = CB // PARTS
    pairs = [(x_hbm.at[pl.ds(p * part * W, part * W)], x_ref.at[pl.ds(p * part * W, part * W)]) for p in range(PARTS)]
    pairs += [(good_hbm, good_ref), (resp_hbm, resp_ref), (table_hbm, table_ref)]
    copies = [pltpu.make_async_copy(source, target, sems.at[at]) for at, (source, target) in enumerate(pairs)]
    for copy in copies:
        copy.start()
    lanes = S // 128
    for p in range(PARTS):
        copies[p].wait()
        rows = pl.ds(p * part * W, part * W)
        for lane in range(lanes):
            xs[lane, rows, :] = x_ref[rows, 128 * lane : 128 * (lane + 1)].astype(jnp.float32)
        for w in range(W):
            rows = pl.ds(p * part * W + w, part, stride=W)
            v = jnp.concatenate([xs[lane, rows, :] for lane in range(lanes)], axis=1)
            power = jnp.mean(v * v, axis=-1, keepdims=True)
            scaled = (v * lax.rsqrt(power + 1e-06)).astype(jnp.bfloat16)
            normed[pl.ds(w * CB + p * part, part), :] = scaled
    for copy in copies[PARTS:]:
        copy.wait()
    gain = jnp.transpose(jnp.broadcast_to(resp_ref[...], (2 * CB, F)))
    low = low_lanes(F)
    good = good_ref[...].astype(jnp.float32)
    for half in range(2):
        rows = normed[pl.ds(half * 4 * CB, 4 * CB), :]
        spectra = lax.dot_general(
            table_ref[...], rows, (((1,), (1,)), ((), ())), preferred_element_type=jnp.float32
        )
        for pair in range(2):
            w = 4 * half + 2 * pair
            mask = jnp.concatenate([good[w : w + 1, :], good[w + 1 : w + 2, :]], axis=1)
            weight = gain * mask
            cols = slice(2 * CB * pair, 2 * CB * (pair + 1))
            re = spectra[:F, cols] * weight
            im = spectra[F:, cols] * weight
            first = jnp.where(low, re, turn(im)).astype(jnp.bfloat16).reshape(DAYS, FS, 2 * CB)
            second = jnp.where(low, turn(re), im).astype(jnp.bfloat16).reshape(DAYS, FS, 2 * CB)
            for to in range(2):
                out_ref[to, :, w] = first
                out_ref[to, :, w + 1] = second


def cross_into(out_ref, left, right):
    low = low_lanes(DAYS * W)
    blank = jnp.zeros((2 * DAYS * W, 2 * CB), jnp.bfloat16)
    for pair in range(FS // 2):
        rows = [pl.ds(2 * pair + f, DAYS * W, stride=FS) for f in range(2)]
        one, other = (left[r, :] for r in rows)
        both = [jnp.where(low, one, turn(other)), jnp.where(low, turn(one), other)]
        both = jnp.transpose(jnp.concatenate(both, axis=0)).astype(jnp.bfloat16)
        parts = []
        for r in rows:
            two = right[r, :]
            parts.append(jnp.concatenate([jnp.where(low, two, -two), turn(two)], axis=0).astype(jnp.bfloat16))
        parts = [jnp.concatenate([parts[0], blank], axis=1), jnp.concatenate([blank, parts[1]], axis=1)]
        cross = jnp.dot(
            jnp.concatenate([both[:CB], both[CB:]], axis=1), jnp.concatenate(parts, axis=0),
            preferred_element_type=jnp.float32,
        )
        for k in range(DAYS):
            rows = slice(8 * k, 8 * k + 8)
            piece = jnp.concatenate([cross[rows, : 2 * CB], cross[rows, 2 * CB :]], axis=0)
            out_ref[k, pl.ds(16 * pair, 16), :] = piece.astype(jnp.bfloat16)


def second_kernel(odd_ref, near_ref, swap_ref, out_ref, left, right):
    @pl.when(odd_ref[0] == 1)
    def _():
        left[...] = swap_ref[...].astype(jnp.float32)
        right[...] = near_ref[1].astype(jnp.float32)

    @pl.when(odd_ref[0] == 0)
    def _():
        left[...] = near_ref[0].astype(jnp.float32)
        right[...] = swap_ref[...].astype(jnp.float32)

    cross_into(out_ref, left, right)


def first_kernel(odd_ref, near_ref, swap_ref, out_ref, left, right):
    @pl.when(odd_ref[0] == 1)
    def _():
        left[...] = near_ref[0].astype(jnp.float32)
        right[...] = near_ref[1].astype(jnp.float32)

    @pl.when(odd_ref[0] == 0)
    def _():
        left[...] = near_ref[1].astype(jnp.float32)
        right[...] = swap_ref[...].astype(jnp.float32)

    cross_into(out_ref, left, right)


def lags_of(wide, table):
    bins = wide.shape[0] // 8
    low = low_lanes(bins)
    for pair in range(4):
        one, two = (wide[pl.ds(2 * pair + i, bins, stride=8), :] for i in range(2))
        re = jnp.where(low, one, turn(two))
        im = jnp.where(low, turn(one), two)
        yield pl.ds(2 * pair, 2), lax.dot_general(
            jnp.concatenate([re, im], axis=0).astype(jnp.bfloat16), table,
            (((0,), (0,)), ((), ())), preferred_element_type=jnp.float32,
        ).reshape(2, CB, L)


def lag_kernel(cross_ref, table_ref, out_ref, wide):
    wide[...] = cross_ref[...].astype(jnp.float32)
    for rows, lags in lags_of(wide, table_ref[...]):
        out_ref[rows] = lags.astype(out_ref.dtype)


def join_kernel(first_ref, second_ref, out_ref):
    out_ref[:, 0] = first_ref[...]
    out_ref[:, 1] = second_ref[...].astype(jnp.float32)


def call(kernel, out_shape, dtype, scratch, flops, *args, scalars=0, space=pltpu.VMEM, limit=VMEM):
    smem = [pl.BlockSpec(memory_space=pltpu.SMEM)] * scalars
    if dtype is not None:
        out_shape = jax.ShapeDtypeStruct(out_shape, dtype)
    return pl.pallas_call(
        kernel,
        out_shape=out_shape,
        in_specs=smem + [pl.BlockSpec(memory_space=space)] * (len(args) - scalars),
        out_specs=jax.tree.map(lambda _: pl.BlockSpec(memory_space=pltpu.VMEM), out_shape),
        scratch_shapes=scratch,
        compiler_params=pltpu.CompilerParams(vmem_limit_bytes=limit),
        cost_estimate=pl.CostEstimate(flops=flops, bytes_accessed=2 << 20, transcendentals=0),
    )(*args)


WHOLE = pltpu.VMEM((ROWS, 2 * CB), jnp.float32)
UNIT_FLOPS = 2 * 64 * 256 * 128
LAG_FLOPS = 2 * 8 * 64 * 512 * 128


def spectra_call(x, good, response):
    operands = (x, good, response, jnp.asarray(dft_table()))
    scratch = [pltpu.VMEM(v.shape, v.dtype) for v in operands]
    scratch += [pltpu.VMEM((S // 128, CB * W, 128), jnp.float32), pltpu.VMEM((CB * W, S), jnp.bfloat16)]
    return call(
        spectra_kernel, (2, DAYS, W, FS, 2 * CB), jnp.bfloat16, scratch + [pltpu.SemaphoreType.DMA((PARTS + 3,))],
        2 * CB * W * S * 2 * F, *operands, space=pltpu.HBM, limit=56 * 1024 * 1024,
    )


def exchange(v):
    return lax.all_to_all(v, "day", 0, 0, tiled=True)


def shards(recordings, good_windows, response):
    blocks = lax.axis_size("chan")
    odd = lax.rem(lax.axis_index("chan"), 2)
    flag = odd.astype(jnp.int32).reshape(1)
    x = recordings.reshape(CB * W, S)
    good = jnp.transpose(good_windows, (0, 2, 1)).reshape(W, CB)
    table = jnp.asarray(lag_table())
    spectra = spectra_call(x, good, response.reshape(1, F))
    groups = [
        [b % blocks * DAYS + d for b in (block, block + 1) for d in range(DAYS)]
        for block in range(1, blocks, 2)
    ]
    near = lax.all_to_all(
        spectra.reshape(2 * DAYS, W, FS, 2 * CB), ("chan", "day"), 0, 0, axis_index_groups=groups, tiled=True
    ).reshape(2, ROWS, 2 * CB)
    mine = jnp.where(odd == 1, near[0], near[1])
    swap = lax.ppermute(mine, "chan", [(b, b ^ 1) for b in range(blocks)])

    def cross(kernel):
        return call(
            kernel, (DAYS, FS * 8, 2 * CB), jnp.bfloat16, [WHOLE] * 2, FS * UNIT_FLOPS, flag, near, swap, scalars=1
        )

    def lags(pairs, dtype):
        return call(
            lag_kernel, (8, CB, L), dtype, [WHOLE], LAG_FLOPS, pairs.reshape(F * 8, 2 * CB), table
        )

    second = exchange(cross(second_kernel))
    first = exchange(cross(first_kernel))
    second = lags(second, jnp.bfloat16)
    second = lax.ppermute(second, "chan", [(b, (b - 1) % blocks) for b in range(blocks)])
    first = lags(first, jnp.float32)
    return call(join_kernel, (8, 2, CB, L), jnp.float32, [], 1 << 17, first, second)


def solution(mesh):
    in_specs = (P("day", "chan", None, None), P("day", "chan", None), P())
    out_specs = P(("chan", "day"), None, None, None)
    return jax.shard_map(shards, mesh=mesh, in_specs=in_specs, out_specs=out_specs, check_vma=False)
```

```python
import math

import jax
import jax.numpy as jnp
import ml_dtypes
import numpy as np
from jax import lax
from jax.experimental import pallas as pl
from jax.experimental.pallas import tpu as pltpu
from jax.sharding import PartitionSpec as P

FIRST_BIN = 4
S = 1024
F = 256
L = 128
CB = 64
W = 8
DAYS = 8
FS = F // DAYS
ROWS = DAYS * W * FS
VMEM = 24 * 1024 * 1024
PARTS = 4


def phase_table(product):
    phase = np.mod(product, S).astype(np.float32) * np.float32(2.0 * math.pi / S)
    return np.concatenate([np.cos(phase), -np.sin(phase)], axis=0).astype(ml_dtypes.bfloat16)


def dft_table():
    return phase_table((np.arange(F) + FIRST_BIN)[:, None] * np.arange(S)[None, :])


def lag_table():
    return phase_table((np.arange(F) + FIRST_BIN)[:, None] * (np.arange(L) - L // 2)[None, :])


def low_lanes(rows):
    return lax.broadcasted_iota(jnp.int32, (rows, 2 * CB), 1) < CB


def turn(v):
    return pltpu.roll(v, CB, 1)


def spectra_kernel(x_hbm, good_hbm, resp_hbm, table_hbm, out_ref, x_ref, good_ref, resp_ref, table_ref, xs, normed, sems):
    part = CB // PARTS
    pairs = [(x_hbm.at[pl.ds(p * part * W, part * W)], x_ref.at[pl.ds(p * part * W, part * W)]) for p in range(PARTS)]
    pairs += [(good_hbm, good_ref), (resp_hbm, resp_ref), (table_hbm, table_ref)]
    copies = [pltpu.make_async_copy(source, target, sems.at[at]) for at, (source, target) in enumerate(pairs)]
    for copy in copies:
        copy.start()
    lanes = S // 128
    for p in range(PARTS):
        copies[p].wait()
        rows = pl.ds(p * part * W, part * W)
        for lane in range(lanes):
            xs[lane, rows, :] = x_ref[rows, 128 * lane : 128 * (lane + 1)].astype(jnp.float32)
        for w in range(W):
            rows = pl.ds(p * part * W + w, part, stride=W)
            v = jnp.concatenate([xs[lane, rows, :] for lane in range(lanes)], axis=1)
            power = jnp.mean(v * v, axis=-1, keepdims=True)
            scaled = (v * lax.rsqrt(power + 1e-06)).astype(jnp.bfloat16)
            normed[pl.ds(w * CB + p * part, part), :] = scaled
    for copy in copies[PARTS:]:
        copy.wait()
    gain = jnp.transpose(jnp.broadcast_to(resp_ref[...], (2 * CB, F)))
    low = low_lanes(F)
    good = good_ref[...].astype(jnp.float32)
    for half in range(2):
        rows = normed[pl.ds(half * 4 * CB, 4 * CB), :]
        spectra = lax.dot_general(
            table_ref[...], rows, (((1,), (1,)), ((), ())), preferred_element_type=jnp.float32
        )
        for pair in range(2):
            w = 4 * half + 2 * pair
            mask = jnp.concatenate([good[w : w + 1, :], good[w + 1 : w + 2, :]], axis=1)
            weight = gain * mask
            cols = slice(2 * CB * pair, 2 * CB * (pair + 1))
            re = spectra[:F, cols] * weight
            im = spectra[F:, cols] * weight
            first = jnp.where(low, re, turn(im)).astype(jnp.bfloat16).reshape(DAYS, FS, 2 * CB)
            second = jnp.where(low, turn(re), im).astype(jnp.bfloat16).reshape(DAYS, FS, 2 * CB)
            for to in range(2):
                out_ref[to, :, w] = first
                out_ref[to, :, w + 1] = second


def left_of(ref, pair):
    low = low_lanes(DAYS * W)
    one, other = (ref[pl.ds(2 * pair + f, DAYS * W, stride=FS), :] for f in range(2))
    both = [jnp.where(low, one, turn(other)), jnp.where(low, turn(one), other)]
    both = jnp.transpose(jnp.concatenate(both, axis=0)).astype(jnp.bfloat16)
    return jnp.concatenate([both[:CB], both[CB:]], axis=1)


def right_of(ref, pair):
    low = low_lanes(DAYS * W)
    parts = []
    for f in range(2):
        two = ref[pl.ds(2 * pair + f, DAYS * W, stride=FS), :]
        parts.append(jnp.concatenate([jnp.where(low, two, -two), turn(two)], axis=0).astype(jnp.bfloat16))
    return parts


def cross_into(out_ref, left, right):
    blank = jnp.zeros((2 * DAYS * W, 2 * CB), jnp.bfloat16)
    for pair in range(FS // 2):
        one, two = right(pair)
        parts = [jnp.concatenate([one, blank], axis=1), jnp.concatenate([blank, two], axis=1)]
        cross = jnp.dot(left(pair), jnp.concatenate(parts, axis=0), preferred_element_type=jnp.float32)
        for k in range(DAYS):
            rows = slice(8 * k, 8 * k + 8)
            piece = jnp.concatenate([cross[rows, : 2 * CB], cross[rows, 2 * CB :]], axis=0)
            out_ref[k, pl.ds(16 * pair, 16), :] = piece.astype(jnp.bfloat16)


def ready_kernel(odd_ref, near_ref, left_ref, right_ref, wide):
    @pl.when(odd_ref[0] == 1)
    def _():
        wide[...] = near_ref[1].astype(jnp.float32)
        for pair in range(FS // 2):
            for f, part in enumerate(right_of(wide, pair)):
                right_ref[2 * pair + f] = part

    @pl.when(odd_ref[0] == 0)
    def _():
        wide[...] = near_ref[0].astype(jnp.float32)
        for pair in range(FS // 2):
            left_ref[pair] = left_of(wide, pair)


def second_kernel(odd_ref, left_ref, right_ref, swap_ref, out_ref, wide):
    wide[...] = swap_ref[...].astype(jnp.float32)

    @pl.when(odd_ref[0] == 1)
    def _():
        cross_into(
            out_ref, lambda pair: left_of(wide, pair), lambda pair: (right_ref[2 * pair], right_ref[2 * pair + 1])
        )

    @pl.when(odd_ref[0] == 0)
    def _():
        cross_into(out_ref, lambda pair: left_ref[pair], lambda pair: right_of(wide, pair))


def first_kernel(odd_ref, near_ref, swap_ref, out_ref, left, right):
    @pl.when(odd_ref[0] == 1)
    def _():
        left[...] = near_ref[0].astype(jnp.float32)
        right[...] = near_ref[1].astype(jnp.float32)

    @pl.when(odd_ref[0] == 0)
    def _():
        left[...] = near_ref[1].astype(jnp.float32)
        right[...] = swap_ref[...].astype(jnp.float32)

    cross_into(out_ref, lambda pair: left_of(left, pair), lambda pair: right_of(right, pair))


def lags_of(wide, table):
    bins = wide.shape[0] // 8
    low = low_lanes(bins)
    for pair in range(4):
        one, two = (wide[pl.ds(2 * pair + i, bins, stride=8), :] for i in range(2))
        re = jnp.where(low, one, turn(two))
        im = jnp.where(low, turn(one), two)
        yield pl.ds(2 * pair, 2), lax.dot_general(
            jnp.concatenate([re, im], axis=0).astype(jnp.bfloat16), table,
            (((0,), (0,)), ((), ())), preferred_element_type=jnp.float32,
        ).reshape(2, CB, L)


def lag_kernel(cross_ref, table_ref, out_ref, wide):
    wide[...] = cross_ref[...].astype(jnp.float32)
    for rows, lags in lags_of(wide, table_ref[...]):
        out_ref[rows] = lags.astype(out_ref.dtype)


def first_lag_kernel(cross_ref, table_ref, out_hbm, wide, stage, sems):
    wide[...] = cross_ref[...].astype(jnp.float32)
    copies = []
    for at, (rows, lags) in enumerate(lags_of(wide, table_ref[...])):
        stage[rows] = lags
        copies.append(pltpu.make_async_copy(stage.at[rows], out_hbm.at[rows, 0], sems.at[at]))
        copies[-1].start()
    for copy in copies:
        copy.wait()


def second_into_kernel(second_ref, held_hbm, out_hbm, stage, sem):
    stage[...] = second_ref[...].astype(jnp.float32)
    copy = pltpu.make_async_copy(stage, out_hbm.at[:, 1], sem)
    copy.start()
    copy.wait()


def call(kernel, out_shape, dtype, scratch, flops, *args, scalars=0, space=pltpu.VMEM, out_space=pltpu.VMEM, limit=VMEM):
    smem = [pl.BlockSpec(memory_space=pltpu.SMEM)] * scalars
    return pl.pallas_call(
        kernel,
        out_shape=jax.ShapeDtypeStruct(out_shape, dtype),
        in_specs=smem + [pl.BlockSpec(memory_space=space)] * (len(args) - scalars),
        out_specs=pl.BlockSpec(memory_space=out_space),
        scratch_shapes=scratch,
        compiler_params=pltpu.CompilerParams(vmem_limit_bytes=limit),
        cost_estimate=pl.CostEstimate(flops=flops, bytes_accessed=2 << 20, transcendentals=0),
    )(*args)


WHOLE = pltpu.VMEM((ROWS, 2 * CB), jnp.float32)
UNIT_FLOPS = 2 * 64 * 256 * 128
LAG_FLOPS = 2 * 8 * 64 * 512 * 128


def spectra_call(x, good, response):
    operands = (x, good, response, jnp.asarray(dft_table()))
    scratch = [pltpu.VMEM(v.shape, v.dtype) for v in operands]
    scratch += [pltpu.VMEM((S // 128, CB * W, 128), jnp.float32), pltpu.VMEM((CB * W, S), jnp.bfloat16)]
    return call(
        spectra_kernel, (2, DAYS, W, FS, 2 * CB), jnp.bfloat16, scratch + [pltpu.SemaphoreType.DMA((PARTS + 3,))],
        2 * CB * W * S * 2 * F, *operands, space=pltpu.HBM, limit=56 * 1024 * 1024,
    )


def exchange(v):
    return lax.all_to_all(v, "day", 0, 0, tiled=True)


def shards(recordings, good_windows, response):
    blocks = lax.axis_size("chan")
    odd = lax.rem(lax.axis_index("chan"), 2)
    flag = odd.astype(jnp.int32).reshape(1)
    x = recordings.reshape(CB * W, S)
    good = jnp.transpose(good_windows, (0, 2, 1)).reshape(W, CB)
    table = jnp.asarray(lag_table())
    spectra = spectra_call(x, good, response.reshape(1, F))
    groups = [
        [b % blocks * DAYS + d for b in (block, block + 1) for d in range(DAYS)]
        for block in range(1, blocks, 2)
    ]
    near = lax.all_to_all(
        spectra.reshape(2 * DAYS, W, FS, 2 * CB), ("chan", "day"), 0, 0, axis_index_groups=groups, tiled=True
    ).reshape(2, ROWS, 2 * CB)
    mine = jnp.where(odd == 1, near[0], near[1])
    swap = lax.ppermute(mine, "chan", [(b, b ^ 1) for b in range(blocks)])

    shape = (DAYS, FS * 8, 2 * CB)
    left, right = pl.pallas_call(
        ready_kernel,
        out_shape=[
            jax.ShapeDtypeStruct((FS // 2, CB, 4 * CB), jnp.bfloat16),
            jax.ShapeDtypeStruct((FS, 2 * CB, 2 * CB), jnp.bfloat16),
        ],
        in_specs=[pl.BlockSpec(memory_space=pltpu.SMEM), pl.BlockSpec(memory_space=pltpu.VMEM)],
        out_specs=[pl.BlockSpec(memory_space=pltpu.VMEM)] * 2,
        scratch_shapes=[WHOLE],
        compiler_params=pltpu.CompilerParams(vmem_limit_bytes=VMEM),
        cost_estimate=pl.CostEstimate(flops=1 << 20, bytes_accessed=2 << 20, transcendentals=0),
    )(flag, near)
    second = exchange(
        call(
            second_kernel, shape, jnp.bfloat16, [WHOLE], FS * UNIT_FLOPS, flag, left, right, swap, scalars=1
        )
    )
    first = exchange(
        call(first_kernel, shape, jnp.bfloat16, [WHOLE] * 2, FS * UNIT_FLOPS, flag, near, swap, scalars=1)
    )

    second = call(
        lag_kernel, (8, CB, L), jnp.bfloat16, [WHOLE], LAG_FLOPS, second.reshape(F * 8, 2 * CB), table
    )
    second = lax.ppermute(second, "chan", [(b, (b - 1) % blocks) for b in range(blocks)])
    stage = pltpu.VMEM((8, CB, L), jnp.float32)
    first = call(
        first_lag_kernel, (8, 2, CB, L), jnp.float32, [WHOLE, stage, pltpu.SemaphoreType.DMA((4,))], LAG_FLOPS,
        first.reshape(F * 8, 2 * CB), table, out_space=pltpu.HBM,
    )
    return pl.pallas_call(
        second_into_kernel,
        out_shape=jax.ShapeDtypeStruct((8, 2, CB, L), jnp.float32),
        in_specs=[pl.BlockSpec(memory_space=pltpu.VMEM), pl.BlockSpec(memory_space=pltpu.HBM)],
        out_specs=pl.BlockSpec(memory_space=pltpu.HBM),
        scratch_shapes=[stage, pltpu.SemaphoreType.DMA],
        input_output_aliases={1: 0},
        compiler_params=pltpu.CompilerParams(vmem_limit_bytes=VMEM),
        cost_estimate=pl.CostEstimate(flops=1 << 17, bytes_accessed=1 << 18, transcendentals=0),
    )(second, first)


def solution(mesh):
    in_specs = (P("day", "chan", None, None), P("day", "chan", None), P())
    out_specs = P(("chan", "day"), None, None, None)
    return jax.shard_map(shards, mesh=mesh, in_specs=in_specs, out_specs=out_specs, check_vma=False)
```

```python
import math

import jax
import jax.numpy as jnp
import ml_dtypes
import numpy as np
from jax import lax
from jax.experimental import pallas as pl
from jax.experimental.pallas import tpu as pltpu
from jax.sharding import PartitionSpec as P

FIRST_BIN = 4
S = 1024
F = 256
L = 128
CB = 64
W = 8
DAYS = 8
FS = F // DAYS
ROWS = DAYS * W * FS
VMEM = 24 * 1024 * 1024
PARTS = 4


def phase_table(product):
    phase = np.mod(product, S).astype(np.float32) * np.float32(2.0 * math.pi / S)
    return np.concatenate([np.cos(phase), -np.sin(phase)], axis=0).astype(ml_dtypes.bfloat16)


def dft_table():
    return phase_table((np.arange(F) + FIRST_BIN)[:, None] * np.arange(S)[None, :])


def lag_table():
    return phase_table((np.arange(F) + FIRST_BIN)[:, None] * (np.arange(L) - L // 2)[None, :])


def low_lanes(rows):
    return lax.broadcasted_iota(jnp.int32, (rows, 2 * CB), 1) < CB


def turn(v):
    return pltpu.roll(v, CB, 1)


def spectra_kernel(x_hbm, good_hbm, resp_hbm, table_hbm, out_ref, x_ref, good_ref, resp_ref, table_ref, xs, normed, sems):
    part = CB // PARTS
    pairs = [(x_hbm.at[pl.ds(p * part * W, part * W)], x_ref.at[pl.ds(p * part * W, part * W)]) for p in range(PARTS)]
    pairs += [(good_hbm, good_ref), (resp_hbm, resp_ref), (table_hbm, table_ref.at[:, pl.ds(0, S // 2)])]
    copies = [pltpu.make_async_copy(source, target, sems.at[at]) for at, (source, target) in enumerate(pairs)]
    for copy in copies:
        copy.start()
    lanes = S // 128
    for p in range(PARTS):
        copies[p].wait()
        rows = pl.ds(p * part * W, part * W)
        for lane in range(lanes):
            xs[lane, rows, :] = x_ref[rows, 128 * lane : 128 * (lane + 1)].astype(jnp.float32)
        for w in range(W):
            rows = pl.ds(p * part * W + w, part, stride=W)
            v = jnp.concatenate([xs[lane, rows, :] for lane in range(lanes)], axis=1)
            power = jnp.mean(v * v, axis=-1, keepdims=True)
            scaled = (v * lax.rsqrt(power + 1e-06)).astype(jnp.bfloat16)
            normed[pl.ds(w * CB + p * part, part), :] = scaled
    for copy in copies[PARTS:]:
        copy.wait()
    half = table_ref[:, : S // 2]
    flip = lax.broadcasted_iota(jnp.int32, half.shape, 0) % 2 == 1
    table_ref[:, S // 2 :] = jnp.where(flip, -half.astype(jnp.float32), half.astype(jnp.float32)).astype(jnp.bfloat16)
    gain = jnp.transpose(jnp.broadcast_to(resp_ref[...], (2 * CB, F)))
    low = low_lanes(F)
    good = good_ref[...].astype(jnp.float32)
    for half in range(2):
        rows = normed[pl.ds(half * 4 * CB, 4 * CB), :]
        spectra = lax.dot_general(
            table_ref[...], rows, (((1,), (1,)), ((), ())), preferred_element_type=jnp.float32
        )
        for pair in range(2):
            w = 4 * half + 2 * pair
            mask = jnp.concatenate([good[w : w + 1, :], good[w + 1 : w + 2, :]], axis=1)
            weight = gain * mask
            cols = slice(2 * CB * pair, 2 * CB * (pair + 1))
            re = spectra[:F, cols] * weight
            im = spectra[F:, cols] * weight
            first = jnp.where(low, re, turn(im)).astype(jnp.bfloat16).reshape(DAYS, FS, 2 * CB)
            second = jnp.where(low, turn(re), im).astype(jnp.bfloat16).reshape(DAYS, FS, 2 * CB)
            for to in range(2):
                out_ref[to, :, w] = first
                out_ref[to, :, w + 1] = second


def left_of(ref, pair):
    low = low_lanes(DAYS * W)
    one, other = (ref[pl.ds(2 * pair + f, DAYS * W, stride=FS), :] for f in range(2))
    both = [jnp.where(low, one, turn(other)), jnp.where(low, turn(one), other)]
    both = jnp.transpose(jnp.concatenate(both, axis=0)).astype(jnp.bfloat16)
    return jnp.concatenate([both[:CB], both[CB:]], axis=1)


def right_of(ref, pair):
    low = low_lanes(DAYS * W)
    parts = []
    for f in range(2):
        two = ref[pl.ds(2 * pair + f, DAYS * W, stride=FS), :]
        parts.append(jnp.concatenate([jnp.where(low, two, -two), turn(two)], axis=0).astype(jnp.bfloat16))
    return parts


def cross_into(out_ref, left, right):
    blank = jnp.zeros((2 * DAYS * W, 2 * CB), jnp.bfloat16)
    for pair in range(FS // 2):
        one, two = right(pair)
        parts = [jnp.concatenate([one, blank], axis=1), jnp.concatenate([blank, two], axis=1)]
        cross = jnp.dot(left(pair), jnp.concatenate(parts, axis=0), preferred_element_type=jnp.float32)
        for k in range(DAYS):
            rows = slice(8 * k, 8 * k + 8)
            piece = jnp.concatenate([cross[rows, : 2 * CB], cross[rows, 2 * CB :]], axis=0)
            out_ref[k, pl.ds(16 * pair, 16), :] = piece.astype(jnp.bfloat16)


def ready_kernel(odd_ref, near_ref, left_ref, right_ref, wide):
    @pl.when(odd_ref[0] == 1)
    def _():
        wide[...] = near_ref[1].astype(jnp.float32)
        for pair in range(FS // 2):
            for f, part in enumerate(right_of(wide, pair)):
                right_ref[2 * pair + f] = part

    @pl.when(odd_ref[0] == 0)
    def _():
        wide[...] = near_ref[0].astype(jnp.float32)
        for pair in range(FS // 2):
            left_ref[pair] = left_of(wide, pair)


def second_kernel(odd_ref, left_ref, right_ref, swap_ref, out_ref, wide):
    wide[...] = swap_ref[...].astype(jnp.float32)

    @pl.when(odd_ref[0] == 1)
    def _():
        cross_into(
            out_ref, lambda pair: left_of(wide, pair), lambda pair: (right_ref[2 * pair], right_ref[2 * pair + 1])
        )

    @pl.when(odd_ref[0] == 0)
    def _():
        cross_into(out_ref, lambda pair: left_ref[pair], lambda pair: right_of(wide, pair))


def first_kernel(odd_ref, near_ref, swap_ref, out_ref, left, right):
    @pl.when(odd_ref[0] == 1)
    def _():
        left[...] = near_ref[0].astype(jnp.float32)
        right[...] = near_ref[1].astype(jnp.float32)

    @pl.when(odd_ref[0] == 0)
    def _():
        left[...] = near_ref[1].astype(jnp.float32)
        right[...] = swap_ref[...].astype(jnp.float32)

    cross_into(out_ref, lambda pair: left_of(left, pair), lambda pair: right_of(right, pair))


def lags_of(wide, table):
    bins = wide.shape[0] // 8
    low = low_lanes(bins)
    for pair in range(4):
        one, two = (wide[pl.ds(2 * pair + i, bins, stride=8), :] for i in range(2))
        re = jnp.where(low, one, turn(two))
        im = jnp.where(low, turn(one), two)
        yield pl.ds(2 * pair, 2), lax.dot_general(
            jnp.concatenate([re, im], axis=0).astype(jnp.bfloat16), table,
            (((0,), (0,)), ((), ())), preferred_element_type=jnp.float32,
        ).reshape(2, CB, L)


def lag_kernel(cross_ref, table_ref, out_ref, wide):
    wide[...] = cross_ref[...].astype(jnp.float32)
    for rows, lags in lags_of(wide, table_ref[...]):
        out_ref[rows] = lags.astype(out_ref.dtype)


def first_lag_kernel(cross_ref, table_ref, out_hbm, wide, stage, sems):
    wide[...] = cross_ref[...].astype(jnp.float32)
    copies = []
    for at, (rows, lags) in enumerate(lags_of(wide, table_ref[...])):
        stage[rows] = lags
        copies.append(pltpu.make_async_copy(stage.at[rows], out_hbm.at[rows, 0], sems.at[at]))
        copies[-1].start()
    for copy in copies:
        copy.wait()


def second_into_kernel(second_ref, held_hbm, out_hbm, stage, sem):
    stage[...] = second_ref[...].astype(jnp.float32)
    copy = pltpu.make_async_copy(stage, out_hbm.at[:, 1], sem)
    copy.start()
    copy.wait()


def call(kernel, out_shape, dtype, scratch, flops, *args, scalars=0, space=pltpu.VMEM, out_space=pltpu.VMEM, limit=VMEM):
    smem = [pl.BlockSpec(memory_space=pltpu.SMEM)] * scalars
    return pl.pallas_call(
        kernel,
        out_shape=jax.ShapeDtypeStruct(out_shape, dtype),
        in_specs=smem + [pl.BlockSpec(memory_space=space)] * (len(args) - scalars),
        out_specs=pl.BlockSpec(memory_space=out_space),
        scratch_shapes=scratch,
        compiler_params=pltpu.CompilerParams(vmem_limit_bytes=limit),
        cost_estimate=pl.CostEstimate(flops=flops, bytes_accessed=2 << 20, transcendentals=0),
    )(*args)


WHOLE = pltpu.VMEM((ROWS, 2 * CB), jnp.float32)
UNIT_FLOPS = 2 * 64 * 256 * 128
LAG_FLOPS = 2 * 8 * 64 * 512 * 128


def spectra_call(x, good, response):
    operands = (x, good, response, jnp.asarray(dft_table()[:, : S // 2]))
    scratch = [pltpu.VMEM(v.shape, v.dtype) for v in operands[:3]] + [pltpu.VMEM((2 * F, S), jnp.bfloat16)]
    scratch += [pltpu.VMEM((S // 128, CB * W, 128), jnp.float32), pltpu.VMEM((CB * W, S), jnp.bfloat16)]
    return call(
        spectra_kernel, (2, DAYS, W, FS, 2 * CB), jnp.bfloat16, scratch + [pltpu.SemaphoreType.DMA((PARTS + 3,))],
        2 * CB * W * S * 2 * F, *operands, space=pltpu.HBM, limit=56 * 1024 * 1024,
    )


def exchange(v):
    return lax.all_to_all(v, "day", 0, 0, tiled=True)


def shards(recordings, good_windows, response):
    blocks = lax.axis_size("chan")
    odd = lax.rem(lax.axis_index("chan"), 2)
    flag = odd.astype(jnp.int32).reshape(1)
    x = recordings.reshape(CB * W, S)
    good = jnp.transpose(good_windows, (0, 2, 1)).reshape(W, CB)
    table = jnp.asarray(lag_table())
    spectra = spectra_call(x, good, response.reshape(1, F))
    groups = [
        [b % blocks * DAYS + d for b in (block, block + 1) for d in range(DAYS)]
        for block in range(1, blocks, 2)
    ]
    near = lax.all_to_all(
        spectra.reshape(2 * DAYS, W, FS, 2 * CB), ("chan", "day"), 0, 0, axis_index_groups=groups, tiled=True
    ).reshape(2, ROWS, 2 * CB)
    mine = jnp.where(odd == 1, near[0], near[1])
    swap = lax.ppermute(mine, "chan", [(b, b ^ 1) for b in range(blocks)])

    shape = (DAYS, FS * 8, 2 * CB)
    left, right = pl.pallas_call(
        ready_kernel,
        out_shape=[
            jax.ShapeDtypeStruct((FS // 2, CB, 4 * CB), jnp.bfloat16),
            jax.ShapeDtypeStruct((FS, 2 * CB, 2 * CB), jnp.bfloat16),
        ],
        in_specs=[pl.BlockSpec(memory_space=pltpu.SMEM), pl.BlockSpec(memory_space=pltpu.VMEM)],
        out_specs=[pl.BlockSpec(memory_space=pltpu.VMEM)] * 2,
        scratch_shapes=[WHOLE],
        compiler_params=pltpu.CompilerParams(vmem_limit_bytes=VMEM),
        cost_estimate=pl.CostEstimate(flops=1 << 20, bytes_accessed=2 << 20, transcendentals=0),
    )(flag, near)
    second = exchange(
        call(
            second_kernel, shape, jnp.bfloat16, [WHOLE], FS * UNIT_FLOPS, flag, left, right, swap, scalars=1
        )
    )
    first = exchange(
        call(first_kernel, shape, jnp.bfloat16, [WHOLE] * 2, FS * UNIT_FLOPS, flag, near, swap, scalars=1)
    )

    second = call(
        lag_kernel, (8, CB, L), jnp.bfloat16, [WHOLE], LAG_FLOPS, second.reshape(F * 8, 2 * CB), table
    )
    second = lax.ppermute(second, "chan", [(b, (b - 1) % blocks) for b in range(blocks)])
    stage = pltpu.VMEM((8, CB, L), jnp.float32)
    first = call(
        first_lag_kernel, (8, 2, CB, L), jnp.float32, [WHOLE, stage, pltpu.SemaphoreType.DMA((4,))], LAG_FLOPS,
        first.reshape(F * 8, 2 * CB), table, out_space=pltpu.HBM,
    )
    return pl.pallas_call(
        second_into_kernel,
        out_shape=jax.ShapeDtypeStruct((8, 2, CB, L), jnp.float32),
        in_specs=[pl.BlockSpec(memory_space=pltpu.VMEM), pl.BlockSpec(memory_space=pltpu.HBM)],
        out_specs=pl.BlockSpec(memory_space=pltpu.HBM),
        scratch_shapes=[stage, pltpu.SemaphoreType.DMA],
        input_output_aliases={1: 0},
        compiler_params=pltpu.CompilerParams(vmem_limit_bytes=VMEM),
        cost_estimate=pl.CostEstimate(flops=1 << 17, bytes_accessed=1 << 18, transcendentals=0),
    )(second, first)


def solution(mesh):
    in_specs = (P("day", "chan", None, None), P("day", "chan", None), P())
    out_specs = P(("chan", "day"), None, None, None)
    return jax.shard_map(shards, mesh=mesh, in_specs=in_specs, out_specs=out_specs, check_vma=False)
```
